32 devices in a mesh: tr: 4 (over y, x), line: 8 (over z, core).
Axes of the slice: x: 2, y: 2, z: 4, core: 2. Of those that a mesh axis runs over, the one named last changes fastest.
Arguments:
- initial: float32 [32, 512, 512], P('line', 'tr'), may hold values from -96 to 96
- lateral: float32 [32], replicated, may hold values from 0.05 to 0.5
- vertical: float32 [32], replicated, may hold values from 0 to 512, as said below
Outputs:
- heat_field_final: float32 [32, 512, 512], P('line', 'tr')
The draws below stay inside these ranges and needn't reach their ends.
Inputs may be any that keep to these rules, and one draw needn't show every extreme that they name: `vertical`: positive.
All inputs are finite; a program needn't handle non-finite values.
Results may differ from the reference program's by a relative error of at most 0.0003.
Values sent between devices are 32-bit elements; how exact they have to be, the bound alone decides.
A program may use at most 192 MiB of HBM per device.

```python
import math
import jax
import jax.numpy as jnp
from jax import lax

NX = 512
NY = 512
CZ = 4
NODES = 4
NZ = 32


def draw_vertical(key, part):
    angle_key, rough_key = jax.random.split(jax.random.fold_in(key, 11))
    angle_shift = jax.random.uniform(angle_key, (), jnp.float32, 0.0, 2.0 * math.pi)
    cell_index = jnp.arange(NZ, dtype=jnp.float32)
    smooth_part = math.log(16.0) * jnp.cos(2.0 * math.pi / NZ * cell_index + angle_shift)
    rough_part = jax.random.uniform(rough_key, (NZ,), jnp.float32, -math.log(2.0), math.log(2.0))
    return CZ * CZ * jnp.exp(smooth_part + rough_part)


def shard_levels(key, dims, shards, low, high):
    factor_of = 1.0
    for dim, blocks in shards:
        draws = jax.random.uniform(jax.random.fold_in(jax.random.fold_in(key, 6), dim), (blocks,), jnp.float32, low / len(shards), high / len(shards))
        factor_of = factor_of * jnp.repeat(jnp.exp(draws), dims[dim] // blocks).reshape((-1,) + (1,) * (len(dims) - 1 - dim))
    return factor_of


def noise(stream_key, shape, spread, most, pieces=(), held_as=jnp.bfloat16):
    loudness = shard_levels(stream_key, shape, pieces, -0.22, 0.18) if pieces else 1.0
    values = jax.random.normal(stream_key, shape, jnp.float32) * spread * loudness
    return jnp.minimum(jnp.maximum(values, -most), most).astype(held_as)


def setup_inputs(seed: int = 0) -> dict:
    key_list = jax.random.split(jax.random.key(seed), 4)
    initial = noise(key_list[0], (NZ, NX, NY), 16.0, 96.0, ((0, 8), (1, 4)), jnp.float32)
    lateral = jnp.clip(jnp.exp(jax.random.uniform(key_list[1], (NZ,), jnp.float32, math.log(0.05), math.log(0.5))), 0.05, 0.5)
    vertical = draw_vertical(jax.random.fold_in(key_list[3], 71), 0)
    return dict(initial=initial, lateral=lateral, vertical=vertical)


final_time = 1.0


def talbot_nodes(node_count):
    radius = 2.0 * node_count / (5.0 * final_time)
    result = [(radius, 0.0, 0.5 * radius / node_count * math.exp(radius * final_time), 0.0)]
    for number in range(1, node_count):
        node_angle = number * math.pi / node_count
        cotangent = math.cos(node_angle) / math.sin(node_angle)
        shift_real = radius * node_angle * cotangent
        shift_imag = radius * node_angle
        sigma_term = node_angle + (node_angle * cotangent - 1.0) * cotangent
        magnitude = radius / node_count * math.exp(final_time * shift_real)
        exp_real = magnitude * math.cos(final_time * shift_imag)
        exp_imag = magnitude * math.sin(final_time * shift_imag)
        result.append((shift_real, shift_imag, exp_real - exp_imag * sigma_term, exp_imag + exp_real * sigma_term))
    return result


def cyclic_lines(spectrum, shift_value, lam_values, lateral, vertical):
    cell_count = spectrum.shape[0]
    lower_faces = jnp.roll(vertical, 1)
    corner = -vertical[cell_count - 1]
    gamma_value = -(shift_value + lateral[0] * lam_values + lower_faces[0] + vertical[0])
    positions = jnp.arange(cell_count)
    first_flags = positions == 0
    last_flags = positions == cell_count - 1
    zeros = jnp.zeros_like(spectrum[0])

    def forward(carry, row_data):
        c_prev, y_prev, q_prev = carry
        lateral_row, lower_face, upper_face, rhs_row, first_flag, last_flag = row_data
        diagonal = shift_value + lateral_row * lam_values + lower_face + upper_face
        diagonal = diagonal - jnp.where(first_flag, gamma_value, zeros)
        diagonal = diagonal - jnp.where(last_flag, corner * corner / gamma_value, zeros)
        extra_rhs = jnp.where(first_flag, gamma_value, zeros) + jnp.where(last_flag, corner + zeros, zeros)
        pivot_value = diagonal + lower_face * c_prev
        c_next = -upper_face / pivot_value
        y_next = (rhs_row + lower_face * y_prev) / pivot_value
        q_next = (extra_rhs + lower_face * q_prev) / pivot_value
        return (c_next, y_next, q_next), (c_next, y_next, q_next)

    _, stored = lax.scan(forward, (zeros, zeros, zeros),
                         (lateral, lower_faces, vertical, spectrum, first_flags, last_flags))

    def backward(carry, row_data):
        y_after, q_after = carry
        c_row, y_row, q_row = row_data
        y_value = y_row - c_row * y_after
        q_value = q_row - c_row * q_after
        return (y_value, q_value), (y_value, q_value)

    _, (y_solved, q_solved) = lax.scan(backward, (zeros, zeros), stored, reverse=True)
    ratio = corner / gamma_value
    dot_y = y_solved[0] + ratio * y_solved[cell_count - 1]
    dot_q = q_solved[0] + ratio * q_solved[cell_count - 1]
    return y_solved - (dot_y / (1.0 + dot_q))[None] * q_solved


def reference(initial, lateral, vertical):
    cell_count, x_width, y_width = initial.shape
    spectrum = jnp.fft.fft2(initial, axes=(1, 2))
    lam_x = 4.0 * jnp.sin(math.pi * jnp.arange(x_width) / x_width) ** 2
    lam_y = 4.0 * jnp.sin(math.pi * jnp.arange(y_width) / y_width) ** 2
    lam_values = lam_x[:, None] + lam_y[None, :]
    total = jnp.zeros_like(spectrum)
    for shift_real, shift_imag, weight_real, weight_imag in talbot_nodes(NODES):
        solved = cyclic_lines(spectrum, shift_real + 1j * shift_imag, lam_values, lateral, vertical)
        total = total + (weight_real + 1j * weight_imag) * solved
    return jnp.real(jnp.fft.ifft2(total, axes=(1, 2))).astype(jnp.float32)
```

```python
import functools
import math

import jax
import jax.numpy as jnp
import numpy as np
from jax import lax
from jax.experimental import pallas as pl
from jax.experimental.pallas import tpu as pltpu
from jax.sharding import PartitionSpec as P

NODES = 4
final_time = 1.0
AXES = ("line", "tr")


def talbot_nodes(node_count):
    radius = 2.0 * node_count / (5.0 * final_time)
    result = [(radius, 0.0, 0.5 * radius / node_count * math.exp(radius * final_time), 0.0)]
    for number in range(1, node_count):
        node_angle = number * math.pi / node_count
        cotangent = math.cos(node_angle) / math.sin(node_angle)
        shift_real = radius * node_angle * cotangent
        shift_imag = radius * node_angle
        sigma_term = node_angle + (node_angle * cotangent - 1.0) * cotangent
        magnitude = radius / node_count * math.exp(final_time * shift_real)
        exp_real = magnitude * math.cos(final_time * shift_imag)
        exp_imag = magnitude * math.sin(final_time * shift_imag)
        result.append(
            (
                shift_real,
                shift_imag,
                exp_real - exp_imag * sigma_term,
                exp_imag + exp_real * sigma_term,
            )
        )
    return result


def hartley(length):
    index = np.arange(length)
    angles = 2.0 * math.pi / length * ((index[:, None] * index[None, :]) % length)
    return np.cos(angles) + np.sin(angles)


def mode_values(length):
    return 4.0 * np.sin(math.pi / length * np.arange(length)) ** 2


def times(left, right):
    lr, li = left
    rr, ri = right
    if li is None and ri is None:
        return (lr * rr, None)
    if li is None:
        return (lr * rr, lr * ri)
    if ri is None:
        return (lr * rr, li * rr)
    return (lr * rr - li * ri, lr * ri + li * rr)


def plus(left, right):
    lr, li = left
    rr, ri = right
    if li is None:
        return (lr + rr, ri)
    if ri is None:
        return (lr + rr, li)
    return (lr + rr, li + ri)


def scaled(factor, value):
    return (factor * value[0], None if value[1] is None else factor * value[1])


def inverse(value):
    real, imag = value
    if imag is None:
        return (1.0 / real, None)
    norm = 1.0 / (real * real + imag * imag)
    return (real * norm, -imag * norm)


def slots(node):
    return (0, None) if node == 0 else (2 * node - 1, 2 * node)


def load(ref, node, z):
    real, imag = slots(node)
    return (ref[real, z], None if imag is None else ref[imag, z])


def store(ref, node, z, value):
    real, imag = slots(node)
    ref[real, z] = value[0]
    if imag is not None:
        ref[imag, z] = value[1]


PLANES = 2 * NODES - 1


def factor(lam, lat, vert, inv_ref, resp_ref):
    layers = resp_ref.shape[1]
    last = layers - 1
    nodes = talbot_nodes(NODES)
    shifts = [(n[0], None if k == 0 else n[1]) for k, n in enumerate(nodes)]

    def diagonal(z, below):
        base = lat[z] * lam + (below + vert[z])
        return [(base + s[0], None if s[1] is None else s[1] + jnp.zeros_like(lam)) for s in shifts]

    below = vert[last]
    carry = []
    for k, d in enumerate(diagonal(0, below)):
        inv = inverse(d)
        g = (below + jnp.zeros_like(lam), None)
        if k:
            g = (g[0], jnp.zeros_like(lam))
        store(inv_ref, k, 0, inv)
        store(resp_ref, k, 0, g)
        carry.append((inv, times(inv, g)))

    def flat(items):
        return tuple(jax.tree.leaves(items))

    tree = jax.tree.structure(carry)

    def forward(z, leaves):
        items = jax.tree.unflatten(tree, leaves)
        below = vert[z - 1]
        fresh = []
        for k, d in enumerate(diagonal(z, below)):
            inv, resp = items[k]
            inv = inverse(plus(d, scaled(-(below * below), inv)))
            g = scaled(below, resp)
            store(inv_ref, k, z, inv)
            store(resp_ref, k, z, g)
            fresh.append((inv, times(inv, g)))
        return flat(fresh)

    lax.fori_loop(1, last, forward, flat(carry))
    ones = jnp.ones_like(lam)
    start = [(ones, None if k == 0 else jnp.zeros_like(lam)) for k in range(NODES)]
    tree_up = jax.tree.structure(start)

    def upward(step, leaves):
        items = jax.tree.unflatten(tree_up, leaves)
        z = last - 1 - step
        above = vert[z]
        fresh = []
        for k in range(NODES):
            g = plus(load(resp_ref, k, z), scaled(above, items[k]))
            value = times(load(inv_ref, k, z), g)
            store(resp_ref, k, z, value)
            fresh.append(value)
        return flat(fresh)

    lax.fori_loop(0, last, upward, flat(start))
    for k, d in enumerate(diagonal(last, vert[last - 1])):
        d = plus(d, scaled(-vert[last - 1], load(resp_ref, k, last - 1)))
        d = plus(d, scaled(-vert[last], load(resp_ref, k, 0)))
        store(resp_ref, k, last, inverse(d))


def solve(src, dst, scale, vert, inv_ref, resp_ref, half_ref):
    layers = resp_ref.shape[1]
    last = layers - 1
    nodes = talbot_nodes(NODES)
    weights = [(n[2] * scale, n[3] * scale) for n in nodes]
    zero = jnp.zeros(src.shape[1:], jnp.float32)
    start = [(zero, None if k == 0 else zero) for k in range(NODES)]
    tree = jax.tree.structure(start)

    def flat(items):
        return tuple(jax.tree.leaves(items))

    def gather(z, leaves):
        items = jax.tree.unflatten(tree, leaves)
        value = (src[z], None)
        return flat([plus(items[k], times(load(resp_ref, k, z), value)) for k in range(NODES)])

    sums = jax.tree.unflatten(tree, lax.fori_loop(0, last, gather, flat(start)))
    rhs = src[last]
    roots = [times(load(resp_ref, k, last), plus(sums[k], (rhs, None))) for k in range(NODES)]

    def real_total(items):
        total = weights[0][0] * items[0][0]
        for k in range(1, NODES):
            total = total + weights[k][0] * items[k][0] - weights[k][1] * items[k][1]
        return total

    dst[last] = real_total(roots)

    def forward(z, leaves):
        items = jax.tree.unflatten(tree, leaves)
        below = vert[lax.select(z == 0, last, z - 1)]
        value = (src[z], None)
        fresh = []
        for k in range(NODES):
            g = plus(scaled(below, items[k]), value)
            store(half_ref, k, z, g)
            fresh.append(times(load(inv_ref, k, z), g))
        return flat(fresh)

    lax.fori_loop(0, last, forward, flat(roots))

    def downward(step, leaves):
        items = jax.tree.unflatten(tree, leaves)
        z = last - 1 - step
        above = vert[z]
        fresh = []
        for k in range(NODES):
            g = plus(load(half_ref, k, z), scaled(above, items[k]))
            fresh.append(times(load(inv_ref, k, z), g))
        dst[z] = real_total(fresh)
        return flat(fresh)

    lax.fori_loop(0, last, downward, flat(roots))


def solve_kernel(scale, src, lam, lat, vert, dst, inv_ref, resp_ref, half_ref):
    factor(lam[...], lat, vert, inv_ref, resp_ref)
    solve(src, dst, scale, vert, inv_ref, resp_ref, half_ref)


def vertical_solves(source, lam, lateral, vertical, scale):
    layers, rows, width = source.shape
    plane = (PLANES, layers, rows, width)
    return pl.pallas_call(
        functools.partial(solve_kernel, scale),
        out_shape=jax.ShapeDtypeStruct(source.shape, jnp.float32),
        in_specs=[pl.BlockSpec(memory_space=pltpu.VMEM)] * 2
        + [pl.BlockSpec(memory_space=pltpu.SMEM)] * 2,
        out_specs=pl.BlockSpec(memory_space=pltpu.VMEM),
        scratch_shapes=[pltpu.VMEM(plane, jnp.float32)] * 3,
        compiler_params=pltpu.CompilerParams(vmem_limit_bytes=50 * 1024 * 1024),
    )(source, lam, lateral, vertical)


def plain_path(initial, lateral, vertical):
    z_cells, x_local, y_width = initial.shape
    tr_count, line_count = lax.axis_size("tr"), lax.axis_size("line")
    peers = tr_count * line_count
    x_width = x_local * tr_count
    layers = z_cells * line_count
    y_local = y_width // peers
    high = lax.Precision.HIGH
    along_y = jnp.asarray(hartley(y_width), jnp.float32)
    along_x = jnp.asarray(hartley(x_width), jnp.float32)
    me = lax.axis_index(AXES)
    modes = jnp.einsum("zxy,qy->zqx", initial, along_y, precision=high)
    modes = modes.reshape(z_cells, peers, y_local, x_local).transpose(1, 0, 2, 3)
    modes = lax.all_to_all(modes, AXES, split_axis=0, concat_axis=0, tiled=True)
    modes = modes.reshape(line_count, tr_count, z_cells, y_local, x_local)
    modes = modes.transpose(0, 2, 3, 1, 4).reshape(layers, y_local, x_width)
    modes = jnp.einsum("zqx,xp->zqp", modes, along_x, precision=high)
    lam_y = lax.dynamic_slice_in_dim(
        jnp.asarray(mode_values(y_width), jnp.float32), me * y_local, y_local
    )
    lam = lam_y[:, None] + jnp.asarray(mode_values(x_width), jnp.float32)[None, :]
    total = vertical_solves(modes, lam, lateral, vertical, 1.0 / (x_width * y_width))
    back = jnp.einsum("zqp,px->zqx", total, along_x, precision=high)
    back = back.reshape(line_count, z_cells, y_local, tr_count, x_local)
    back = back.transpose(0, 3, 1, 2, 4).reshape(peers, z_cells, y_local, x_local)
    back = lax.all_to_all(back, AXES, split_axis=0, concat_axis=0, tiled=True)
    back = back.transpose(1, 0, 2, 3).reshape(z_cells, y_width, x_local)
    return jnp.einsum("zqx,qy->zxy", back, along_y, precision=high)


def solution(mesh):
    in_specs = (P("line", "tr", None), P(), P())
    out_specs = P("line", "tr", None)
    return jax.shard_map(
        plain_path, mesh=mesh, in_specs=in_specs, out_specs=out_specs, check_vma=False
    )
```

```python
import functools
import math

import jax
import jax.numpy as jnp
import numpy as np
from jax import lax
from jax.experimental import pallas as pl
from jax.experimental.pallas import tpu as pltpu
from jax.sharding import PartitionSpec as P

NODES = 4
final_time = 1.0
AXES = ("line", "tr")


def talbot_nodes(node_count):
    radius = 2.0 * node_count / (5.0 * final_time)
    result = [(radius, 0.0, 0.5 * radius / node_count * math.exp(radius * final_time), 0.0)]
    for number in range(1, node_count):
        node_angle = number * math.pi / node_count
        cotangent = math.cos(node_angle) / math.sin(node_angle)
        shift_real = radius * node_angle * cotangent
        shift_imag = radius * node_angle
        sigma_term = node_angle + (node_angle * cotangent - 1.0) * cotangent
        magnitude = radius / node_count * math.exp(final_time * shift_real)
        exp_real = magnitude * math.cos(final_time * shift_imag)
        exp_imag = magnitude * math.sin(final_time * shift_imag)
        result.append(
            (
                shift_real,
                shift_imag,
                exp_real - exp_imag * sigma_term,
                exp_imag + exp_real * sigma_term,
            )
        )
    return result


def hartley(length):
    index = np.arange(length)
    angles = 2.0 * math.pi / length * ((index[:, None] * index[None, :]) % length)
    return np.cos(angles) + np.sin(angles)


def mode_values(length):
    return 4.0 * np.sin(math.pi / length * np.arange(length)) ** 2


def times(left, right):
    lr, li = left
    rr, ri = right
    if li is None and ri is None:
        return (lr * rr, None)
    if li is None:
        return (lr * rr, lr * ri)
    if ri is None:
        return (lr * rr, li * rr)
    return (lr * rr - li * ri, lr * ri + li * rr)


def plus(left, right):
    lr, li = left
    rr, ri = right
    if li is None:
        return (lr + rr, ri)
    if ri is None:
        return (lr + rr, li)
    return (lr + rr, li + ri)


def scaled(factor, value):
    return (factor * value[0], None if value[1] is None else factor * value[1])


def inverse(value):
    real, imag = value
    if imag is None:
        return (1.0 / real, None)
    norm = 1.0 / (real * real + imag * imag)
    return (real * norm, -imag * norm)


def slots(node):
    return (0, None) if node == 0 else (2 * node - 1, 2 * node)


def load(ref, node, z):
    real, imag = slots(node)
    return (ref[real, z], None if imag is None else ref[imag, z])


def store(ref, node, z, value):
    real, imag = slots(node)
    ref[real, z] = value[0]
    if imag is not None:
        ref[imag, z] = value[1]


PLANES = 2 * NODES - 1


def factor(lam, lat, vert, inv_ref, resp_ref):
    layers = resp_ref.shape[1]
    last = layers - 1
    nodes = talbot_nodes(NODES)
    shifts = [(n[0], None if k == 0 else n[1]) for k, n in enumerate(nodes)]

    def diagonal(z, below):
        base = lat[z] * lam + (below + vert[z])
        return [(base + s[0], None if s[1] is None else s[1] + jnp.zeros_like(lam)) for s in shifts]

    below = vert[last]
    carry = []
    for k, d in enumerate(diagonal(0, below)):
        inv = inverse(d)
        g = (below + jnp.zeros_like(lam), None)
        if k:
            g = (g[0], jnp.zeros_like(lam))
        store(inv_ref, k, 0, inv)
        store(resp_ref, k, 0, g)
        carry.append((inv, times(inv, g)))

    def flat(items):
        return tuple(jax.tree.leaves(items))

    tree = jax.tree.structure(carry)

    def forward(z, leaves):
        items = jax.tree.unflatten(tree, leaves)
        below = vert[z - 1]
        fresh = []
        for k, d in enumerate(diagonal(z, below)):
            inv, resp = items[k]
            inv = inverse(plus(d, scaled(-(below * below), inv)))
            g = scaled(below, resp)
            store(inv_ref, k, z, inv)
            store(resp_ref, k, z, g)
            fresh.append((inv, times(inv, g)))
        return flat(fresh)

    lax.fori_loop(1, last, forward, flat(carry))
    ones = jnp.ones_like(lam)
    start = [(ones, None if k == 0 else jnp.zeros_like(lam)) for k in range(NODES)]
    tree_up = jax.tree.structure(start)

    def upward(step, leaves):
        items = jax.tree.unflatten(tree_up, leaves)
        z = last - 1 - step
        above = vert[z]
        fresh = []
        for k in range(NODES):
            g = plus(load(resp_ref, k, z), scaled(above, items[k]))
            value = times(load(inv_ref, k, z), g)
            store(resp_ref, k, z, value)
            fresh.append(value)
        return flat(fresh)

    lax.fori_loop(0, last, upward, flat(start))
    for k, d in enumerate(diagonal(last, vert[last - 1])):
        d = plus(d, scaled(-vert[last - 1], load(resp_ref, k, last - 1)))
        d = plus(d, scaled(-vert[last], load(resp_ref, k, 0)))
        store(resp_ref, k, last, inverse(d))


def solve(src, dst, scale, vert, inv_ref, resp_ref, half_ref):
    layers = resp_ref.shape[1]
    last = layers - 1
    nodes = talbot_nodes(NODES)
    weights = [(n[2] * scale, n[3] * scale) for n in nodes]
    zero = jnp.zeros(src.shape[1:], jnp.float32)
    start = [(zero, None if k == 0 else zero) for k in range(NODES)]
    tree = jax.tree.structure(start)

    def flat(items):
        return tuple(jax.tree.leaves(items))

    def gather(z, leaves):
        items = jax.tree.unflatten(tree, leaves)
        value = (src[z], None)
        return flat([plus(items[k], times(load(resp_ref, k, z), value)) for k in range(NODES)])

    sums = jax.tree.unflatten(tree, lax.fori_loop(0, last, gather, flat(start)))
    rhs = src[last]
    roots = [times(load(resp_ref, k, last), plus(sums[k], (rhs, None))) for k in range(NODES)]

    def real_total(items):
        total = weights[0][0] * items[0][0]
        for k in range(1, NODES):
            total = total + weights[k][0] * items[k][0] - weights[k][1] * items[k][1]
        return total

    dst[last] = real_total(roots)

    def forward(z, leaves):
        items = jax.tree.unflatten(tree, leaves)
        below = vert[lax.select(z == 0, last, z - 1)]
        value = (src[z], None)
        fresh = []
        for k in range(NODES):
            g = plus(scaled(below, items[k]), value)
            store(half_ref, k, z, g)
            fresh.append(times(load(inv_ref, k, z), g))
        return flat(fresh)

    lax.fori_loop(0, last, forward, flat(roots))

    def downward(step, leaves):
        items = jax.tree.unflatten(tree, leaves)
        z = last - 1 - step
        above = vert[z]
        fresh = []
        for k in range(NODES):
            g = plus(load(half_ref, k, z), scaled(above, items[k]))
            fresh.append(times(load(inv_ref, k, z), g))
        dst[z] = real_total(fresh)
        return flat(fresh)

    lax.fori_loop(0, last, downward, flat(roots))


def solve_kernel(scale, src, lam, lat, vert, dst, inv_ref, resp_ref, half_ref):
    factor(lam[...], lat, vert, inv_ref, resp_ref)
    solve(src, dst, scale, vert, inv_ref, resp_ref, half_ref)


def vertical_solves(source, lam, lateral, vertical, scale):
    layers, rows, width = source.shape
    plane = (PLANES, layers, rows, width)
    return pl.pallas_call(
        functools.partial(solve_kernel, scale),
        out_shape=jax.ShapeDtypeStruct(source.shape, jnp.float32),
        in_specs=[pl.BlockSpec(memory_space=pltpu.VMEM)] * 2
        + [pl.BlockSpec(memory_space=pltpu.SMEM)] * 2,
        out_specs=pl.BlockSpec(memory_space=pltpu.VMEM),
        scratch_shapes=[pltpu.VMEM(plane, jnp.float32)] * 3,
        compiler_params=pltpu.CompilerParams(vmem_limit_bytes=50 * 1024 * 1024),
    )(source, lam, lateral, vertical)


def plain_path(initial, lateral, vertical):
    z_cells, x_local, y_width = initial.shape
    tr_count, line_count = lax.axis_size("tr"), lax.axis_size("line")
    peers = tr_count * line_count
    x_width = x_local * tr_count
    layers = z_cells * line_count
    y_local = y_width // peers
    high = lax.Precision.HIGH
    along_y = jnp.asarray(hartley(y_width), jnp.float32)
    along_x = jnp.asarray(hartley(x_width), jnp.float32)
    me = lax.axis_index(AXES)
    modes = jnp.einsum("zxy,qy->zqx", initial, along_y, precision=high)
    modes = modes.reshape(z_cells, peers, y_local, x_local).transpose(1, 0, 2, 3)
    modes = lax.all_to_all(modes, AXES, split_axis=0, concat_axis=0, tiled=True)
    modes = modes.reshape(line_count, tr_count, z_cells, y_local, x_local)
    modes = modes.transpose(0, 2, 3, 1, 4).reshape(layers, y_local, x_width)
    modes = jnp.einsum("zqx,xp->zqp", modes, along_x, precision=high)
    lam_y = lax.dynamic_slice_in_dim(
        jnp.asarray(mode_values(y_width), jnp.float32), me * y_local, y_local
    )
    lam = lam_y[:, None] + jnp.asarray(mode_values(x_width), jnp.float32)[None, :]
    total = vertical_solves(modes, lam, lateral, vertical, 1.0 / (x_width * y_width))
    back = jnp.einsum("zqp,px->zqx", total, along_x, precision=high)
    back = back.reshape(line_count, z_cells, y_local, tr_count, x_local)
    back = back.transpose(0, 3, 1, 2, 4).reshape(peers, z_cells, y_local, x_local)
    back = lax.all_to_all(back, AXES, split_axis=0, concat_axis=0, tiled=True)
    back = back.transpose(1, 0, 2, 3).reshape(z_cells, y_width, x_local)
    return jnp.einsum("zqx,qy->zxy", back, along_y, precision=high)


def split(value):
    high = value.astype(jnp.bfloat16)
    return high, (value - high.astype(jnp.float32)).astype(jnp.bfloat16)


def three_pass(left, right, dims):
    def dot(a, b):
        return lax.dot_general(a, b, (dims, ((), ())), preferred_element_type=jnp.float32)

    return dot(left[0], right[0]) + (dot(left[1], right[0]) + dot(left[0], right[1]))


ROWS = 8


def fused_kernel(
    scale,
    sizes,
    init,
    yh,
    yl,
    xh,
    xl,
    lam_y,
    lam_x,
    lat,
    vert,
    out,
    sent,
    arrived,
    modes,
    solved,
    replies,
    back,
    inv_ref,
    resp_ref,
    half_ref,
    send_sem,
    recv_sem,
):
    line_count, tr_count, chunks = sizes
    peers = line_count * tr_count
    z_cells, x_local, y_width = init.shape
    x_width = x_local * tr_count
    layers = z_cells * line_count
    band = peers * ROWS
    line, tr = lax.axis_index("line"), lax.axis_index("tr")
    me = line * tr_count + tr

    def place(index):
        return {"line": index // tr_count, "tr": lax.rem(index, tr_count)}

    def after(j):
        return lax.rem(me + j, peers)

    def before(j):
        return lax.rem(me + peers - j, peers)

    def block(ref, h, index):
        first = pl.multiple_of((index // tr_count) * z_cells, z_cells)
        column = pl.multiple_of(lax.rem(index, tr_count) * x_local, x_local)
        return ref.at[h, pl.ds(first, z_cells), :, pl.ds(column, x_local)]

    def rows(ref, h, index):
        return ref.at[h, :, pl.ds(pl.multiple_of(index * ROWS, ROWS), ROWS), :]

    def forth(h, src_index, dst_index, j):
        return pltpu.make_async_remote_copy(
            src_ref=rows(sent, h, dst_index),
            dst_ref=block(arrived, h, src_index),
            send_sem=send_sem.at[0, h, j],
            recv_sem=recv_sem.at[0, h, j],
            device_id=place(dst_index),
            device_id_type=pl.DeviceIdType.MESH,
        )

    def reply(h, src_index, dst_index, j):
        return pltpu.make_async_remote_copy(
            src_ref=block(replies, h, dst_index),
            dst_ref=rows(back, h, src_index),
            send_sem=send_sem.at[1, h, j],
            recv_sem=recv_sem.at[1, h, j],
            device_id=place(dst_index),
            device_id_type=pl.DeviceIdType.MESH,
        )

    def start_all(make, h):
        @pl.loop(1, peers)
        def _(j):
            make(h, me, after(j), j).start()

    def receive_all(make, h):
        @pl.loop(1, peers)
        def _(j):
            make(h, before(j), me, j).wait_recv()

    def sent_all(make, h):
        @pl.loop(1, peers)
        def _(j):
            make(h, me, after(j), j).wait_send()

    barrier = pltpu.get_barrier_semaphore()

    @pl.loop(1, peers)
    def _(j):
        pl.semaphore_signal(
            barrier, inc=1, device_id=place(after(j)), device_id_type=pl.DeviceIdType.MESH
        )

    source = split(init[...].reshape(z_cells * x_local, y_width))
    for h in range(chunks):
        part = (yh[pl.ds(h * band, band), :], yl[pl.ds(h * band, band), :])
        spectrum = three_pass(part, source, ((1,), (1,)))
        for z in range(z_cells):
            sent[h, z] = spectrum[:, z * x_local : (z + 1) * x_local]
        if h == 0:
            pl.semaphore_wait(barrier, peers - 1)
        start_all(forth, h)
    for h in range(chunks):
        block(arrived, h, me)[...] = rows(sent, h, me)[...]
    for h in range(chunks):
        first = pl.multiple_of(h * band + me * ROWS, ROWS)
        lam = lam_y[pl.ds(first, ROWS), :] + lam_x[...]
        factor(lam, lat, vert, inv_ref.at[h], resp_ref.at[h])
    x_pair = (xh[...], xl[...])
    for h in range(chunks):
        receive_all(forth, h)
        flat = split(arrived[h].reshape(layers * ROWS, x_width))
        modes[...] = three_pass(flat, x_pair, ((1,), (0,))).reshape(layers, ROWS, x_width)
        solve(modes, solved, scale, vert, inv_ref.at[h], resp_ref.at[h], half_ref)
        flat = split(solved[...].reshape(layers * ROWS, x_width))
        replies[h] = three_pass(flat, x_pair, ((1,), (0,))).reshape(layers, ROWS, x_width)
        start_all(reply, h)
        rows(back, h, me)[...] = block(replies, h, me)[...]
    for h in range(chunks):
        receive_all(reply, h)
        part = (yh[pl.ds(h * band, band), :], yl[pl.ds(h * band, band), :])
        wide = jnp.concatenate([back[h, z] for z in range(z_cells)], axis=1)
        field = three_pass(split(wide.T), part, ((1,), (0,)))
        field = field.reshape(z_cells, x_local, y_width)
        if h == 0:
            out[...] = field
        else:
            out[...] += field
    for h in range(chunks):
        sent_all(forth, h)
        sent_all(reply, h)


def halves(matrix):
    single = np.asarray(matrix, np.float32)
    high = single.astype(jnp.bfloat16)
    return high, (single - high.astype(np.float32)).astype(jnp.bfloat16)


def fused_path(initial, lateral, vertical):
    z_cells, x_local, y_width = initial.shape
    tr_count, line_count = lax.axis_size("tr"), lax.axis_size("line")
    peers = tr_count * line_count
    x_width = x_local * tr_count
    layers = z_cells * line_count
    chunks = y_width // (peers * ROWS)
    yh, yl = halves(hartley(y_width))
    xh, xl = halves(hartley(x_width))
    lam_y = np.asarray(mode_values(y_width), np.float32)[:, None]
    lam_x = np.asarray(mode_values(x_width), np.float32)[None, :]
    vmem = pl.BlockSpec(memory_space=pltpu.VMEM)
    smem = pl.BlockSpec(memory_space=pltpu.SMEM)
    f32 = jnp.float32
    narrow = pltpu.VMEM((chunks, z_cells, peers * ROWS, x_local), f32)
    whole = pltpu.VMEM((chunks, layers, ROWS, x_width), f32)
    one = pltpu.VMEM((layers, ROWS, x_width), f32)
    planes = pltpu.VMEM((chunks, PLANES, layers, ROWS, x_width), f32)
    return pl.pallas_call(
        functools.partial(
            fused_kernel, 1.0 / (x_width * y_width), (line_count, tr_count, chunks)
        ),
        out_shape=jax.ShapeDtypeStruct(initial.shape, f32),
        in_specs=[vmem] * 7 + [smem] * 2,
        out_specs=vmem,
        scratch_shapes=[
            narrow,
            whole,
            one,
            one,
            whole,
            narrow,
            planes,
            planes,
            pltpu.VMEM((PLANES, layers, ROWS, x_width), f32),
            pltpu.SemaphoreType.DMA((2, chunks, peers)),
            pltpu.SemaphoreType.DMA((2, chunks, peers)),
        ],
        compiler_params=pltpu.CompilerParams(
            collective_id=0, has_side_effects=True, vmem_limit_bytes=50 * 1024 * 1024
        ),
        cost_estimate=pl.CostEstimate(
            flops=24 * z_cells * x_local * y_width * y_width,
            bytes_accessed=12 * z_cells * x_local * y_width,
            transcendentals=0,
        ),
    )(
        initial,
        *[jnp.asarray(a) for a in (yh, yl, xh, xl, lam_y, lam_x)],
        lateral,
        vertical,
    )


def local(initial, lateral, vertical):
    z_cells, x_local, y_width = initial.shape
    peers = lax.axis_size("tr") * lax.axis_size("line")
    if x_local % 128 == 0 and y_width % (peers * ROWS) == 0:
        return fused_path(initial, lateral, vertical)
    return plain_path(initial, lateral, vertical)


def solution(mesh):
    in_specs = (P("line", "tr", None), P(), P())
    out_specs = P("line", "tr", None)
    return jax.shard_map(
        local, mesh=mesh, in_specs=in_specs, out_specs=out_specs, check_vma=False
    )
```

```python
import functools
import math

import jax
import jax.numpy as jnp
import numpy as np
from jax import lax
from jax.experimental import pallas as pl
from jax.experimental.pallas import tpu as pltpu
from jax.sharding import PartitionSpec as P

NODES = 4
final_time = 1.0
AXES = ("line", "tr")


def talbot_nodes(node_count):
    radius = 2.0 * node_count / (5.0 * final_time)
    result = [(radius, 0.0, 0.5 * radius / node_count * math.exp(radius * final_time), 0.0)]
    for number in range(1, node_count):
        node_angle = number * math.pi / node_count
        cotangent = math.cos(node_angle) / math.sin(node_angle)
        shift_real = radius * node_angle * cotangent
        shift_imag = radius * node_angle
        sigma_term = node_angle + (node_angle * cotangent - 1.0) * cotangent
        magnitude = radius / node_count * math.exp(final_time * shift_real)
        exp_real = magnitude * math.cos(final_time * shift_imag)
        exp_imag = magnitude * math.sin(final_time * shift_imag)
        result.append(
            (
                shift_real,
                shift_imag,
                exp_real - exp_imag * sigma_term,
                exp_imag + exp_real * sigma_term,
            )
        )
    return result


def hartley(length):
    index = np.arange(length)
    angles = 2.0 * math.pi / length * ((index[:, None] * index[None, :]) % length)
    return np.cos(angles) + np.sin(angles)


def mode_values(length):
    return 4.0 * np.sin(math.pi / length * np.arange(length)) ** 2


def times(left, right):
    lr, li = left
    rr, ri = right
    if li is None and ri is None:
        return (lr * rr, None)
    if li is None:
        return (lr * rr, lr * ri)
    if ri is None:
        return (lr * rr, li * rr)
    return (lr * rr - li * ri, lr * ri + li * rr)


def plus(left, right):
    lr, li = left
    rr, ri = right
    if li is None:
        return (lr + rr, ri)
    if ri is None:
        return (lr + rr, li)
    return (lr + rr, li + ri)


def scaled(factor, value):
    return (factor * value[0], None if value[1] is None else factor * value[1])


def inverse(value):
    real, imag = value
    if imag is None:
        return (1.0 / real, None)
    norm = 1.0 / (real * real + imag * imag)
    return (real * norm, -imag * norm)


def slots(node):
    return (0, None) if node == 0 else (2 * node - 1, 2 * node)


def load(ref, node, z):
    real, imag = slots(node)
    return (ref[real, z], None if imag is None else ref[imag, z])


def store(ref, node, z, value):
    real, imag = slots(node)
    ref[real, z] = value[0]
    if imag is not None:
        ref[imag, z] = value[1]


PLANES = 2 * NODES - 1


def factor(lam, lat, vert, inv_ref, resp_ref):
    layers = resp_ref.shape[1]
    last = layers - 1
    nodes = talbot_nodes(NODES)
    shifts = [(n[0], None if k == 0 else n[1]) for k, n in enumerate(nodes)]

    def diagonal(z, below):
        base = lat[z] * lam + (below + vert[z])
        return [(base + s[0], None if s[1] is None else s[1] + jnp.zeros_like(lam)) for s in shifts]

    below = vert[last]
    carry = []
    for k, d in enumerate(diagonal(0, below)):
        inv = inverse(d)
        g = (below + jnp.zeros_like(lam), None)
        if k:
            g = (g[0], jnp.zeros_like(lam))
        store(inv_ref, k, 0, inv)
        store(resp_ref, k, 0, g)
        carry.append((inv, times(inv, g)))

    def flat(items):
        return tuple(jax.tree.leaves(items))

    tree = jax.tree.structure(carry)

    def forward(z, leaves):
        items = jax.tree.unflatten(tree, leaves)
        below = vert[z - 1]
        fresh = []
        for k, d in enumerate(diagonal(z, below)):
            inv, resp = items[k]
            inv = inverse(plus(d, scaled(-(below * below), inv)))
            g = scaled(below, resp)
            store(inv_ref, k, z, inv)
            store(resp_ref, k, z, g)
            fresh.append((inv, times(inv, g)))
        return flat(fresh)

    lax.fori_loop(1, last, forward, flat(carry))
    ones = jnp.ones_like(lam)
    start = [(ones, None if k == 0 else jnp.zeros_like(lam)) for k in range(NODES)]
    tree_up = jax.tree.structure(start)

    def upward(step, leaves):
        items = jax.tree.unflatten(tree_up, leaves)
        z = last - 1 - step
        above = vert[z]
        fresh = []
        for k in range(NODES):
            g = plus(load(resp_ref, k, z), scaled(above, items[k]))
            value = times(load(inv_ref, k, z), g)
            store(resp_ref, k, z, value)
            fresh.append(value)
        return flat(fresh)

    lax.fori_loop(0, last, upward, flat(start))
    for k, d in enumerate(diagonal(last, vert[last - 1])):
        d = plus(d, scaled(-vert[last - 1], load(resp_ref, k, last - 1)))
        d = plus(d, scaled(-vert[last], load(resp_ref, k, 0)))
        store(resp_ref, k, last, inverse(d))


def solve(src, dst, scale, vert, inv_ref, resp_ref, half_ref):
    layers = resp_ref.shape[1]
    last = layers - 1
    nodes = talbot_nodes(NODES)
    weights = [(n[2] * scale, n[3] * scale) for n in nodes]
    zero = jnp.zeros(src.shape[1:], jnp.float32)
    start = [(zero, None if k == 0 else zero) for k in range(NODES)]
    tree = jax.tree.structure(start)

    def flat(items):
        return tuple(jax.tree.leaves(items))

    def gather(z, leaves):
        items = jax.tree.unflatten(tree, leaves)
        value = (src[z], None)
        return flat([plus(items[k], times(load(resp_ref, k, z), value)) for k in range(NODES)])

    sums = jax.tree.unflatten(tree, lax.fori_loop(0, last, gather, flat(start)))
    rhs = src[last]
    roots = [times(load(resp_ref, k, last), plus(sums[k], (rhs, None))) for k in range(NODES)]

    def real_total(items):
        total = weights[0][0] * items[0][0]
        for k in range(1, NODES):
            total = total + weights[k][0] * items[k][0] - weights[k][1] * items[k][1]
        return total

    dst[last] = real_total(roots)

    def forward(z, leaves):
        items = jax.tree.unflatten(tree, leaves)
        below = vert[lax.select(z == 0, last, z - 1)]
        value = (src[z], None)
        fresh = []
        for k in range(NODES):
            g = plus(scaled(below, items[k]), value)
            store(half_ref, k, z, g)
            fresh.append(times(load(inv_ref, k, z), g))
        return flat(fresh)

    lax.fori_loop(0, last, forward, flat(roots))

    def downward(step, leaves):
        items = jax.tree.unflatten(tree, leaves)
        z = last - 1 - step
        above = vert[z]
        fresh = []
        for k in range(NODES):
            g = plus(load(half_ref, k, z), scaled(above, items[k]))
            fresh.append(times(load(inv_ref, k, z), g))
        dst[z] = real_total(fresh)
        return flat(fresh)

    lax.fori_loop(0, last, downward, flat(roots))


def solve_kernel(scale, src, lam, lat, vert, dst, inv_ref, resp_ref, half_ref):
    factor(lam[...], lat, vert, inv_ref, resp_ref)
    solve(src, dst, scale, vert, inv_ref, resp_ref, half_ref)


def vertical_solves(source, lam, lateral, vertical, scale):
    layers, rows, width = source.shape
    plane = (PLANES, layers, rows, width)
    return pl.pallas_call(
        functools.partial(solve_kernel, scale),
        out_shape=jax.ShapeDtypeStruct(source.shape, jnp.float32),
        in_specs=[pl.BlockSpec(memory_space=pltpu.VMEM)] * 2
        + [pl.BlockSpec(memory_space=pltpu.SMEM)] * 2,
        out_specs=pl.BlockSpec(memory_space=pltpu.VMEM),
        scratch_shapes=[pltpu.VMEM(plane, jnp.float32)] * 3,
        compiler_params=pltpu.CompilerParams(vmem_limit_bytes=50 * 1024 * 1024),
    )(source, lam, lateral, vertical)


def plain_path(initial, lateral, vertical):
    z_cells, x_local, y_width = initial.shape
    tr_count, line_count = lax.axis_size("tr"), lax.axis_size("line")
    peers = tr_count * line_count
    x_width = x_local * tr_count
    layers = z_cells * line_count
    y_local = y_width // peers
    high = lax.Precision.HIGH
    along_y = jnp.asarray(hartley(y_width), jnp.float32)
    along_x = jnp.asarray(hartley(x_width), jnp.float32)
    me = lax.axis_index(AXES)
    modes = jnp.einsum("zxy,qy->zqx", initial, along_y, precision=high)
    modes = modes.reshape(z_cells, peers, y_local, x_local).transpose(1, 0, 2, 3)
    modes = lax.all_to_all(modes, AXES, split_axis=0, concat_axis=0, tiled=True)
    modes = modes.reshape(line_count, tr_count, z_cells, y_local, x_local)
    modes = modes.transpose(0, 2, 3, 1, 4).reshape(layers, y_local, x_width)
    modes = jnp.einsum("zqx,xp->zqp", modes, along_x, precision=high)
    lam_y = lax.dynamic_slice_in_dim(
        jnp.asarray(mode_values(y_width), jnp.float32), me * y_local, y_local
    )
    lam = lam_y[:, None] + jnp.asarray(mode_values(x_width), jnp.float32)[None, :]
    total = vertical_solves(modes, lam, lateral, vertical, 1.0 / (x_width * y_width))
    back = jnp.einsum("zqp,px->zqx", total, along_x, precision=high)
    back = back.reshape(line_count, z_cells, y_local, tr_count, x_local)
    back = back.transpose(0, 3, 1, 2, 4).reshape(peers, z_cells, y_local, x_local)
    back = lax.all_to_all(back, AXES, split_axis=0, concat_axis=0, tiled=True)
    back = back.transpose(1, 0, 2, 3).reshape(z_cells, y_width, x_local)
    return jnp.einsum("zqx,qy->zxy", back, along_y, precision=high)


def split(value):
    high = value.astype(jnp.bfloat16)
    return high, (value - high.astype(jnp.float32)).astype(jnp.bfloat16)


def three_pass(left, right, dims):
    def dot(a, b):
        return lax.dot_general(a, b, (dims, ((), ())), preferred_element_type=jnp.float32)

    return dot(left[0], right[0]) + (dot(left[1], right[0]) + dot(left[0], right[1]))


ROWS = 8


def fused_kernel(
    scale,
    sizes,
    init_hbm,
    y_hbm,
    x_hbm,
    lam_hbm,
    lat_hbm,
    vert_hbm,
    out,
    init,
    y_pair,
    x_pair,
    lam,
    lat,
    vert,
    sent,
    arrived,
    modes,
    solved,
    replies,
    back,
    inv_ref,
    resp_ref,
    half_ref,
    load_sem,
    send_sem,
    recv_sem,
):
    line_count, tr_count, chunks = sizes
    peers = line_count * tr_count
    z_cells, x_local, y_width = init.shape
    x_width = x_local * tr_count
    layers = z_cells * line_count
    band = peers * ROWS
    line, tr = lax.axis_index("line"), lax.axis_index("tr")
    me = line * tr_count + tr
    side = line_count // 2

    def loading(place, source, target):
        return pltpu.make_async_copy(source, target, load_sem.at[place])

    first_loads = [loading(0, init_hbm, init), loading(1, y_hbm, y_pair)]
    later_loads = [loading(2, lat_hbm, lat), loading(3, vert_hbm, vert)]
    for h in range(chunks):
        own = pl.multiple_of(h * band + me * ROWS, ROWS)
        later_loads.append(loading(4 + h, lam_hbm.at[pl.ds(own, ROWS), :], lam.at[h]))
    if x_hbm is y_hbm:
        x_pair = y_pair
    else:
        later_loads.append(loading(4 + chunks, x_hbm, x_pair))
    for copy in first_loads + later_loads:
        copy.start()

    def place(index):
        return {"line": index // tr_count, "tr": lax.rem(index, tr_count)}

    def moved(j, sign):
        flip, rest = j // (side * tr_count), lax.rem(j, side * tr_count)
        step, turn = rest // tr_count, lax.rem(rest, tr_count)
        half = lax.rem(line // side + flip, 2)
        spot = lax.rem(lax.rem(line, side) + side + sign * step, side)
        return (half * side + spot) * tr_count + lax.rem(tr + tr_count + sign * turn, tr_count)

    def after(j):
        return moved(j, 1)

    def before(j):
        return moved(j, -1)

    def block(ref, h, index):
        first = pl.multiple_of((index // tr_count) * z_cells, z_cells)
        column = pl.multiple_of(lax.rem(index, tr_count) * x_local, x_local)
        return ref.at[h, pl.ds(first, z_cells), :, pl.ds(column, x_local)]

    def rows(ref, h, index):
        return ref.at[h, :, pl.ds(pl.multiple_of(index * ROWS, ROWS), ROWS), :]

    def forth(h, src_index, dst_index, j):
        return pltpu.make_async_remote_copy(
            src_ref=rows(sent, h, dst_index),
            dst_ref=block(arrived, h, src_index),
            send_sem=send_sem.at[0, h, j],
            recv_sem=recv_sem.at[0, h, j],
            device_id=place(dst_index),
            device_id_type=pl.DeviceIdType.MESH,
        )

    def reply(h, src_index, dst_index, j):
        return pltpu.make_async_remote_copy(
            src_ref=block(replies, h, dst_index),
            dst_ref=rows(back, h, src_index),
            send_sem=send_sem.at[1, h, j],
            recv_sem=recv_sem.at[1, h, j],
            device_id=place(dst_index),
            device_id_type=pl.DeviceIdType.MESH,
        )

    def start_all(make, h):
        @pl.loop(1, peers)
        def _(i):
            j = peers - i
            make(h, me, after(j), j).start()

    def receive_all(make, h):
        @pl.loop(1, peers)
        def _(j):
            make(h, before(j), me, j).wait_recv()

    def sent_all(make, h):
        @pl.loop(1, peers)
        def _(j):
            make(h, me, after(j), j).wait_send()

    barrier = pltpu.get_barrier_semaphore()

    @pl.loop(1, peers)
    def _(j):
        pl.semaphore_signal(
            barrier, inc=1, device_id=place(after(j)), device_id_type=pl.DeviceIdType.MESH
        )

    for copy in first_loads:
        copy.wait()
    source = split(init[...].reshape(z_cells * x_local, y_width))
    for h in range(chunks):
        part = (y_pair[0, pl.ds(h * band, band), :], y_pair[1, pl.ds(h * band, band), :])
        spectrum = three_pass(part, source, ((1,), (1,)))
        for z in range(z_cells):
            sent[h, z] = spectrum[:, z * x_local : (z + 1) * x_local]
        if h == 0:
            pl.semaphore_wait(barrier, peers - 1)
        start_all(forth, h)
    for h in range(chunks):
        block(arrived, h, me)[...] = rows(sent, h, me)[...]
    for copy in later_loads:
        copy.wait()
    for h in range(chunks):
        factor(lam[h], lat, vert, inv_ref.at[h], resp_ref.at[h])
    x_pair = (x_pair[0], x_pair[1])
    for h in range(chunks):
        receive_all(forth, h)
        flat = split(arrived[h].reshape(layers * ROWS, x_width))
        modes[...] = three_pass(flat, x_pair, ((1,), (0,))).reshape(layers, ROWS, x_width)
        solve(modes, solved, scale, vert, inv_ref.at[h], resp_ref.at[h], half_ref)
        flat = split(solved[...].reshape(layers * ROWS, x_width))
        replies[h] = three_pass(flat, x_pair, ((1,), (0,))).reshape(layers, ROWS, x_width)
        start_all(reply, h)
        rows(back, h, me)[...] = block(replies, h, me)[...]
    for h in range(chunks):
        receive_all(reply, h)
        part = (y_pair[0, pl.ds(h * band, band), :], y_pair[1, pl.ds(h * band, band), :])
        wide = jnp.concatenate([back[h, z] for z in range(z_cells)], axis=1)
        field = three_pass(split(wide.T), part, ((1,), (0,)))
        field = field.reshape(z_cells, x_local, y_width)
        if h == 0:
            out[...] = field
        else:
            out[...] += field
    for h in range(chunks):
        sent_all(forth, h)
        sent_all(reply, h)


def halves(matrix):
    single = np.asarray(matrix, np.float32)
    high = single.astype(jnp.bfloat16)
    return high, (single - high.astype(np.float32)).astype(jnp.bfloat16)


def fused_path(initial, lateral, vertical):
    z_cells, x_local, y_width = initial.shape
    tr_count, line_count = lax.axis_size("tr"), lax.axis_size("line")
    peers = tr_count * line_count
    x_width = x_local * tr_count
    layers = z_cells * line_count
    chunks = y_width // (peers * ROWS)
    y_pair = np.stack(halves(hartley(y_width)))
    matrices = [jnp.asarray(y_pair)]
    if x_width != y_width:
        matrices.append(jnp.asarray(np.stack(halves(hartley(x_width)))))
    lam = mode_values(y_width)[:, None] + mode_values(x_width)[None, :]
    f32 = jnp.float32
    scratch_x = (2, x_width, x_width) if x_width != y_width else (2, 16, 128)
    narrow = pltpu.VMEM((chunks, z_cells, peers * ROWS, x_local), f32)
    whole = pltpu.VMEM((chunks, layers, ROWS, x_width), f32)
    one = pltpu.VMEM((layers, ROWS, x_width), f32)
    planes = pltpu.VMEM((chunks, PLANES, layers, ROWS, x_width), f32)
    body = functools.partial(
        fused_kernel, 1.0 / (x_width * y_width), (line_count, tr_count, chunks)
    )

    def kernel(init, y_ref, *rest):
        if len(matrices) == 1:
            rest = (y_ref,) + rest
        body(init, y_ref, *rest)

    return pl.pallas_call(
        kernel,
        out_shape=jax.ShapeDtypeStruct(initial.shape, f32),
        in_specs=[pl.BlockSpec(memory_space=pltpu.HBM)] * (4 + len(matrices)),
        out_specs=pl.BlockSpec(memory_space=pltpu.VMEM),
        scratch_shapes=[
            pltpu.VMEM(initial.shape, f32),
            pltpu.VMEM(y_pair.shape, jnp.bfloat16),
            pltpu.VMEM(scratch_x, jnp.bfloat16),
            pltpu.VMEM((chunks, ROWS, x_width), f32),
            pltpu.SMEM((layers,), f32),
            pltpu.SMEM((layers,), f32),
            narrow,
            whole,
            one,
            one,
            whole,
            narrow,
            planes,
            planes,
            pltpu.VMEM((PLANES, layers, ROWS, x_width), f32),
            pltpu.SemaphoreType.DMA((5 + chunks,)),
            pltpu.SemaphoreType.DMA((2, chunks, peers)),
            pltpu.SemaphoreType.DMA((2, chunks, peers)),
        ],
        compiler_params=pltpu.CompilerParams(
            collective_id=0, has_side_effects=True, vmem_limit_bytes=60 * 1024 * 1024
        ),
        cost_estimate=pl.CostEstimate(
            flops=24 * z_cells * x_local * y_width * y_width,
            bytes_accessed=12 * z_cells * x_local * y_width,
            transcendentals=0,
        ),
    )(
        initial,
        *matrices,
        jnp.asarray(lam, f32),
        lateral,
        vertical,
    )


def local(initial, lateral, vertical):
    z_cells, x_local, y_width = initial.shape
    peers = lax.axis_size("tr") * lax.axis_size("line")
    even = lax.axis_size("line") % 2 == 0
    if even and x_local % 128 == 0 and y_width % (peers * ROWS) == 0:
        return fused_path(initial, lateral, vertical)
    return plain_path(initial, lateral, vertical)


def solution(mesh):
    in_specs = (P("line", "tr", None), P(), P())
    out_specs = P("line", "tr", None)
    return jax.shard_map(
        local, mesh=mesh, in_specs=in_specs, out_specs=out_specs, check_vma=False
    )
```

```python
import functools
import math

import jax
import jax.numpy as jnp
import numpy as np
from jax import lax
from jax.experimental import pallas as pl
from jax.experimental.pallas import tpu as pltpu
from jax.sharding import PartitionSpec as P

NODES = 4
final_time = 1.0
AXES = ("line", "tr")


def talbot_nodes(node_count):
    radius = 2.0 * node_count / (5.0 * final_time)
    result = [(radius, 0.0, 0.5 * radius / node_count * math.exp(radius * final_time), 0.0)]
    for number in range(1, node_count):
        node_angle = number * math.pi / node_count
        cotangent = math.cos(node_angle) / math.sin(node_angle)
        shift_real = radius * node_angle * cotangent
        shift_imag = radius * node_angle
        sigma_term = node_angle + (node_angle * cotangent - 1.0) * cotangent
        magnitude = radius / node_count * math.exp(final_time * shift_real)
        exp_real = magnitude * math.cos(final_time * shift_imag)
        exp_imag = magnitude * math.sin(final_time * shift_imag)
        result.append(
            (
                shift_real,
                shift_imag,
                exp_real - exp_imag * sigma_term,
                exp_imag + exp_real * sigma_term,
            )
        )
    return result


def hartley(length):
    index = np.arange(length)
    angles = 2.0 * math.pi / length * ((index[:, None] * index[None, :]) % length)
    return np.cos(angles) + np.sin(angles)


def mode_values(length):
    return 4.0 * np.sin(math.pi / length * np.arange(length)) ** 2


def times(left, right):
    lr, li = left
    rr, ri = right
    if li is None and ri is None:
        return (lr * rr, None)
    if li is None:
        return (lr * rr, lr * ri)
    if ri is None:
        return (lr * rr, li * rr)
    return (lr * rr - li * ri, lr * ri + li * rr)


def plus(left, right):
    lr, li = left
    rr, ri = right
    if li is None:
        return (lr + rr, ri)
    if ri is None:
        return (lr + rr, li)
    return (lr + rr, li + ri)


def scaled(factor, value):
    return (factor * value[0], None if value[1] is None else factor * value[1])


def inverse(value):
    real, imag = value
    if imag is None:
        return (1.0 / real, None)
    norm = 1.0 / (real * real + imag * imag)
    return (real * norm, -imag * norm)


def slots(node):
    return (0, None) if node == 0 else (2 * node - 1, 2 * node)


def load(ref, node, z):
    real, imag = slots(node)
    return (ref[real, z], None if imag is None else ref[imag, z])


def store(ref, node, z, value):
    real, imag = slots(node)
    ref[real, z] = value[0]
    if imag is not None:
        ref[imag, z] = value[1]


PLANES = 2 * NODES - 1


def factor(lam, lat, vert, inv_ref, resp_ref):
    layers = resp_ref.shape[1]
    last = layers - 1
    nodes = talbot_nodes(NODES)
    shifts = [(n[0], None if k == 0 else n[1]) for k, n in enumerate(nodes)]

    def diagonal(z, below):
        base = lat[z] * lam + (below + vert[z])
        return [(base + s[0], None if s[1] is None else s[1] + jnp.zeros_like(lam)) for s in shifts]

    below = vert[last]
    carry = []
    for k, d in enumerate(diagonal(0, below)):
        inv = inverse(d)
        g = (below + jnp.zeros_like(lam), None)
        if k:
            g = (g[0], jnp.zeros_like(lam))
        store(inv_ref, k, 0, inv)
        store(resp_ref, k, 0, g)
        carry.append((inv, times(inv, g)))

    def flat(items):
        return tuple(jax.tree.leaves(items))

    tree = jax.tree.structure(carry)

    def forward(z, leaves):
        items = jax.tree.unflatten(tree, leaves)
        below = vert[z - 1]
        fresh = []
        for k, d in enumerate(diagonal(z, below)):
            inv, resp = items[k]
            inv = inverse(plus(d, scaled(-(below * below), inv)))
            g = scaled(below, resp)
            store(inv_ref, k, z, inv)
            store(resp_ref, k, z, g)
            fresh.append((inv, times(inv, g)))
        return flat(fresh)

    lax.fori_loop(1, last, forward, flat(carry))
    ones = jnp.ones_like(lam)
    start = [(ones, None if k == 0 else jnp.zeros_like(lam)) for k in range(NODES)]
    tree_up = jax.tree.structure(start)

    def upward(step, leaves):
        items = jax.tree.unflatten(tree_up, leaves)
        z = last - 1 - step
        above = vert[z]
        fresh = []
        for k in range(NODES):
            g = plus(load(resp_ref, k, z), scaled(above, items[k]))
            value = times(load(inv_ref, k, z), g)
            store(resp_ref, k, z, value)
            fresh.append(value)
        return flat(fresh)

    lax.fori_loop(0, last, upward, flat(start))
    for k, d in enumerate(diagonal(last, vert[last - 1])):
        d = plus(d, scaled(-vert[last - 1], load(resp_ref, k, last - 1)))
        d = plus(d, scaled(-vert[last], load(resp_ref, k, 0)))
        store(resp_ref, k, last, inverse(d))


def solve(src, dst, scale, vert, inv_ref, resp_ref, half_ref):
    layers = resp_ref.shape[1]
    last = layers - 1
    nodes = talbot_nodes(NODES)
    weights = [(n[2] * scale, n[3] * scale) for n in nodes]
    zero = jnp.zeros(src.shape[1:], jnp.float32)
    start = [(zero, None if k == 0 else zero) for k in range(NODES)]
    tree = jax.tree.structure(start)

    def flat(items):
        return tuple(jax.tree.leaves(items))

    def gather(z, leaves):
        items = jax.tree.unflatten(tree, leaves)
        value = (src[z], None)
        return flat([plus(items[k], times(load(resp_ref, k, z), value)) for k in range(NODES)])

    sums = jax.tree.unflatten(tree, lax.fori_loop(0, last, gather, flat(start)))
    rhs = src[last]
    roots = [times(load(resp_ref, k, last), plus(sums[k], (rhs, None))) for k in range(NODES)]

    def real_total(items):
        total = weights[0][0] * items[0][0]
        for k in range(1, NODES):
            total = total + weights[k][0] * items[k][0] - weights[k][1] * items[k][1]
        return total

    dst[last] = real_total(roots)

    def forward(z, leaves):
        items = jax.tree.unflatten(tree, leaves)
        below = vert[lax.select(z == 0, last, z - 1)]
        value = (src[z], None)
        fresh = []
        for k in range(NODES):
            g = plus(scaled(below, items[k]), value)
            store(half_ref, k, z, g)
            fresh.append(times(load(inv_ref, k, z), g))
        return flat(fresh)

    lax.fori_loop(0, last, forward, flat(roots))

    def downward(step, leaves):
        items = jax.tree.unflatten(tree, leaves)
        z = last - 1 - step
        above = vert[z]
        fresh = []
        for k in range(NODES):
            g = plus(load(half_ref, k, z), scaled(above, items[k]))
            fresh.append(times(load(inv_ref, k, z), g))
        dst[z] = real_total(fresh)
        return flat(fresh)

    lax.fori_loop(0, last, downward, flat(roots))


def solve_kernel(scale, src, lam, lat, vert, dst, inv_ref, resp_ref, half_ref):
    factor(lam[...], lat, vert, inv_ref, resp_ref)
    solve(src, dst, scale, vert, inv_ref, resp_ref, half_ref)


def vertical_solves(source, lam, lateral, vertical, scale):
    layers, rows, width = source.shape
    plane = (PLANES, layers, rows, width)
    return pl.pallas_call(
        functools.partial(solve_kernel, scale),
        out_shape=jax.ShapeDtypeStruct(source.shape, jnp.float32),
        in_specs=[pl.BlockSpec(memory_space=pltpu.VMEM)] * 2
        + [pl.BlockSpec(memory_space=pltpu.SMEM)] * 2,
        out_specs=pl.BlockSpec(memory_space=pltpu.VMEM),
        scratch_shapes=[pltpu.VMEM(plane, jnp.float32)] * 3,
        compiler_params=pltpu.CompilerParams(vmem_limit_bytes=50 * 1024 * 1024),
    )(source, lam, lateral, vertical)


def plain_path(initial, lateral, vertical):
    z_cells, x_local, y_width = initial.shape
    tr_count, line_count = lax.axis_size("tr"), lax.axis_size("line")
    peers = tr_count * line_count
    x_width = x_local * tr_count
    layers = z_cells * line_count
    y_local = y_width // peers
    high = lax.Precision.HIGH
    along_y = jnp.asarray(hartley(y_width), jnp.float32)
    along_x = jnp.asarray(hartley(x_width), jnp.float32)
    me = lax.axis_index(AXES)
    modes = jnp.einsum("zxy,qy->zqx", initial, along_y, precision=high)
    modes = modes.reshape(z_cells, peers, y_local, x_local).transpose(1, 0, 2, 3)
    modes = lax.all_to_all(modes, AXES, split_axis=0, concat_axis=0, tiled=True)
    modes = modes.reshape(line_count, tr_count, z_cells, y_local, x_local)
    modes = modes.transpose(0, 2, 3, 1, 4).reshape(layers, y_local, x_width)
    modes = jnp.einsum("zqx,xp->zqp", modes, along_x, precision=high)
    lam_y = lax.dynamic_slice_in_dim(
        jnp.asarray(mode_values(y_width), jnp.float32), me * y_local, y_local
    )
    lam = lam_y[:, None] + jnp.asarray(mode_values(x_width), jnp.float32)[None, :]
    total = vertical_solves(modes, lam, lateral, vertical, 1.0 / (x_width * y_width))
    back = jnp.einsum("zqp,px->zqx", total, along_x, precision=high)
    back = back.reshape(line_count, z_cells, y_local, tr_count, x_local)
    back = back.transpose(0, 3, 1, 2, 4).reshape(peers, z_cells, y_local, x_local)
    back = lax.all_to_all(back, AXES, split_axis=0, concat_axis=0, tiled=True)
    back = back.transpose(1, 0, 2, 3).reshape(z_cells, y_width, x_local)
    return jnp.einsum("zqx,qy->zxy", back, along_y, precision=high)


def split(value):
    high = value.astype(jnp.bfloat16)
    return high, (value - high.astype(jnp.float32)).astype(jnp.bfloat16)


def three_pass(left, right, dims):
    def dot(a, b):
        return lax.dot_general(a, b, (dims, ((), ())), preferred_element_type=jnp.float32)

    return dot(left[0], right[0]) + (dot(left[1], right[0]) + dot(left[0], right[1]))


ROWS = 8


def fused_kernel(
    scale,
    sizes,
    init_hbm,
    y_hbm,
    x_hbm,
    lam_hbm,
    lat_hbm,
    vert_hbm,
    out,
    init,
    y_pair,
    x_pair,
    lam,
    lat,
    vert,
    sent,
    arrived,
    modes,
    solved,
    replies,
    back,
    inv_ref,
    resp_ref,
    half_ref,
    load_sem,
    send_sem,
    recv_sem,
):
    line_count, tr_count, chunks = sizes
    peers = line_count * tr_count
    z_cells, x_local, y_width = init.shape
    x_width = x_local * tr_count
    layers = z_cells * line_count
    band = peers * ROWS
    line, tr = lax.axis_index("line"), lax.axis_index("tr")
    me = line * tr_count + tr

    def loading(place, source, target):
        return pltpu.make_async_copy(source, target, load_sem.at[place])

    first_loads = [loading(0, init_hbm, init), loading(1, y_hbm, y_pair)]
    later_loads = [loading(2, lat_hbm, lat), loading(3, vert_hbm, vert)]
    for h in range(chunks):
        own = pl.multiple_of(h * band + me * ROWS, ROWS)
        later_loads.append(loading(4 + h, lam_hbm.at[pl.ds(own, ROWS), :], lam.at[h]))
    if x_hbm is y_hbm:
        x_pair = y_pair
    else:
        later_loads.append(loading(4 + chunks, x_hbm, x_pair))
    for copy in first_loads + later_loads:
        copy.start()

    def place(index):
        return {"line": index // tr_count, "tr": lax.rem(index, tr_count)}

    def after(j):
        return lax.rem(me + j, peers)

    def before(j):
        return lax.rem(me + peers - j, peers)

    def block(ref, h, index):
        first = pl.multiple_of((index // tr_count) * z_cells, z_cells)
        column = pl.multiple_of(lax.rem(index, tr_count) * x_local, x_local)
        return ref.at[h, pl.ds(first, z_cells), :, pl.ds(column, x_local)]

    def rows(ref, h, index):
        return ref.at[h, :, pl.ds(pl.multiple_of(index * ROWS, ROWS), ROWS), :]

    def forth(h, src_index, dst_index, j):
        return pltpu.make_async_remote_copy(
            src_ref=rows(sent, h, dst_index),
            dst_ref=block(arrived, h, src_index),
            send_sem=send_sem.at[0, h, j],
            recv_sem=recv_sem.at[0, h, j],
            device_id=place(dst_index),
            device_id_type=pl.DeviceIdType.MESH,
        )

    def reply(h, src_index, dst_index, j):
        return pltpu.make_async_remote_copy(
            src_ref=block(replies, h, dst_index),
            dst_ref=rows(back, h, src_index),
            send_sem=send_sem.at[1, h, j],
            recv_sem=recv_sem.at[1, h, j],
            device_id=place(dst_index),
            device_id_type=pl.DeviceIdType.MESH,
        )

    def start_all(make, h):
        @pl.loop(1, peers)
        def _(j):
            make(h, me, after(j), j).start()

    def receive_all(make, h):
        @pl.loop(1, peers)
        def _(j):
            make(h, before(j), me, j).wait_recv()

    def sent_all(make, h):
        @pl.loop(1, peers)
        def _(j):
            make(h, me, after(j), j).wait_send()

    barrier = pltpu.get_barrier_semaphore()

    @pl.loop(1, peers)
    def _(j):
        pl.semaphore_signal(
            barrier, inc=1, device_id=place(after(j)), device_id_type=pl.DeviceIdType.MESH
        )

    for copy in first_loads:
        copy.wait()
    source = split(init[...].reshape(z_cells * x_local, y_width))
    for h in range(chunks):
        part = (y_pair[0, pl.ds(h * band, band), :], y_pair[1, pl.ds(h * band, band), :])
        spectrum = three_pass(part, source, ((1,), (1,)))
        for z in range(z_cells):
            sent[h, z] = spectrum[:, z * x_local : (z + 1) * x_local]
        if h == 0:
            pl.semaphore_wait(barrier, peers - 1)
        start_all(forth, h)
    for h in range(chunks):
        block(arrived, h, me)[...] = rows(sent, h, me)[...]
    for copy in later_loads:
        copy.wait()
    for h in range(chunks):
        factor(lam[h], lat, vert, inv_ref.at[h], resp_ref.at[h])
    x_pair = (x_pair[0], x_pair[1])
    for h in range(chunks):
        receive_all(forth, h)
        flat = split(arrived[h].reshape(layers * ROWS, x_width))
        modes[...] = three_pass(flat, x_pair, ((1,), (0,))).reshape(layers, ROWS, x_width)
        solve(modes, solved, scale, vert, inv_ref.at[h], resp_ref.at[h], half_ref)
        flat = split(solved[...].reshape(layers * ROWS, x_width))
        replies[h] = three_pass(flat, x_pair, ((1,), (0,))).reshape(layers, ROWS, x_width)
        start_all(reply, h)
        rows(back, h, me)[...] = block(replies, h, me)[...]
    for h in range(chunks):
        receive_all(reply, h)
        part = (y_pair[0, pl.ds(h * band, band), :], y_pair[1, pl.ds(h * band, band), :])
        wide = jnp.concatenate([back[h, z] for z in range(z_cells)], axis=1)
        field = three_pass(split(wide.T), part, ((1,), (0,)))
        field = field.reshape(z_cells, x_local, y_width)
        if h == 0:
            out[...] = field
        else:
            out[...] += field
    for h in range(chunks):
        sent_all(forth, h)
        sent_all(reply, h)


def halves(matrix):
    single = np.asarray(matrix, np.float32)
    high = single.astype(jnp.bfloat16)
    return high, (single - high.astype(np.float32)).astype(jnp.bfloat16)


def fused_path(initial, lateral, vertical):
    z_cells, x_local, y_width = initial.shape
    tr_count, line_count = lax.axis_size("tr"), lax.axis_size("line")
    peers = tr_count * line_count
    x_width = x_local * tr_count
    layers = z_cells * line_count
    chunks = y_width // (peers * ROWS)
    y_pair = np.stack(halves(hartley(y_width)))
    matrices = [jnp.asarray(y_pair)]
    if x_width != y_width:
        matrices.append(jnp.asarray(np.stack(halves(hartley(x_width)))))
    lam = mode_values(y_width)[:, None] + mode_values(x_width)[None, :]
    f32 = jnp.float32
    scratch_x = (2, x_width, x_width) if x_width != y_width else (2, 16, 128)
    narrow = pltpu.VMEM((chunks, z_cells, peers * ROWS, x_local), f32)
    whole = pltpu.VMEM((chunks, layers, ROWS, x_width), f32)
    one = pltpu.VMEM((layers, ROWS, x_width), f32)
    planes = pltpu.VMEM((chunks, PLANES, layers, ROWS, x_width), f32)
    body = functools.partial(
        fused_kernel, 1.0 / (x_width * y_width), (line_count, tr_count, chunks)
    )

    def kernel(init, y_ref, *rest):
        if len(matrices) == 1:
            rest = (y_ref,) + rest
        body(init, y_ref, *rest)

    return pl.pallas_call(
        kernel,
        out_shape=jax.ShapeDtypeStruct(initial.shape, f32),
        in_specs=[pl.BlockSpec(memory_space=pltpu.HBM)] * (4 + len(matrices)),
        out_specs=pl.BlockSpec(memory_space=pltpu.VMEM),
        scratch_shapes=[
            pltpu.VMEM(initial.shape, f32),
            pltpu.VMEM(y_pair.shape, jnp.bfloat16),
            pltpu.VMEM(scratch_x, jnp.bfloat16),
            pltpu.VMEM((chunks, ROWS, x_width), f32),
            pltpu.SMEM((layers,), f32),
            pltpu.SMEM((layers,), f32),
            narrow,
            whole,
            one,
            one,
            whole,
            narrow,
            planes,
            planes,
            pltpu.VMEM((PLANES, layers, ROWS, x_width), f32),
            pltpu.SemaphoreType.DMA((5 + chunks,)),
            pltpu.SemaphoreType.DMA((2, chunks, peers)),
            pltpu.SemaphoreType.DMA((2, chunks, peers)),
        ],
        compiler_params=pltpu.CompilerParams(
            collective_id=0, has_side_effects=True, vmem_limit_bytes=52 * 1024 * 1024
        ),
        cost_estimate=pl.CostEstimate(
            flops=24 * z_cells * x_local * y_width * y_width,
            bytes_accessed=12 * z_cells * x_local * y_width,
            transcendentals=0,
        ),
    )(
        initial,
        *matrices,
        jnp.asarray(lam, f32),
        lateral,
        vertical,
    )


def local(initial, lateral, vertical):
    z_cells, x_local, y_width = initial.shape
    peers = lax.axis_size("tr") * lax.axis_size("line")
    if x_local % 128 == 0 and y_width % (peers * ROWS) == 0:
        return fused_path(initial, lateral, vertical)
    return plain_path(initial, lateral, vertical)


def solution(mesh):
    in_specs = (P("line", "tr", None), P(), P())
    out_specs = P("line", "tr", None)
    return jax.shard_map(
        local, mesh=mesh, in_specs=in_specs, out_specs=out_specs, check_vma=False
    )
```

```python
import functools
import math

import jax
import jax.numpy as jnp
import numpy as np
from jax import lax
from jax.experimental import pallas as pl
from jax.experimental.pallas import tpu as pltpu
from jax.sharding import PartitionSpec as P

NODES = 4
final_time = 1.0
AXES = ("line", "tr")


def talbot_nodes(node_count):
    radius = 2.0 * node_count / (5.0 * final_time)
    result = [(radius, 0.0, 0.5 * radius / node_count * math.exp(radius * final_time), 0.0)]
    for number in range(1, node_count):
        node_angle = number * math.pi / node_count
        cotangent = math.cos(node_angle) / math.sin(node_angle)
        shift_real = radius * node_angle * cotangent
        shift_imag = radius * node_angle
        sigma_term = node_angle + (node_angle * cotangent - 1.0) * cotangent
        magnitude = radius / node_count * math.exp(final_time * shift_real)
        exp_real = magnitude * math.cos(final_time * shift_imag)
        exp_imag = magnitude * math.sin(final_time * shift_imag)
        result.append(
            (
                shift_real,
                shift_imag,
                exp_real - exp_imag * sigma_term,
                exp_imag + exp_real * sigma_term,
            )
        )
    return result


def hartley(length):
    index = np.arange(length)
    angles = 2.0 * math.pi / length * ((index[:, None] * index[None, :]) % length)
    return np.cos(angles) + np.sin(angles)


def mode_values(length):
    return 4.0 * np.sin(math.pi / length * np.arange(length)) ** 2


def times(left, right):
    lr, li = left
    rr, ri = right
    if li is None and ri is None:
        return (lr * rr, None)
    if li is None:
        return (lr * rr, lr * ri)
    if ri is None:
        return (lr * rr, li * rr)
    return (lr * rr - li * ri, lr * ri + li * rr)


def plus(left, right):
    lr, li = left
    rr, ri = right
    if li is None:
        return (lr + rr, ri)
    if ri is None:
        return (lr + rr, li)
    return (lr + rr, li + ri)


def scaled(factor, value):
    return (factor * value[0], None if value[1] is None else factor * value[1])


def inverse(value):
    real, imag = value
    if imag is None:
        return (1.0 / real, None)
    norm = 1.0 / (real * real + imag * imag)
    return (real * norm, -imag * norm)


def slots(node):
    return (0, None) if node == 0 else (2 * node - 1, 2 * node)


def load(ref, node, z):
    real, imag = slots(node)
    return (ref[real, z], None if imag is None else ref[imag, z])


def store(ref, node, z, value):
    real, imag = slots(node)
    ref[real, z] = value[0]
    if imag is not None:
        ref[imag, z] = value[1]


PLANES = 2 * NODES - 1


def factor(lam, lat, vert, inv_ref, resp_ref):
    layers = resp_ref.shape[1]
    last = layers - 1
    nodes = talbot_nodes(NODES)
    shifts = [(n[0], None if k == 0 else n[1]) for k, n in enumerate(nodes)]

    def diagonal(z, below):
        base = lat[z] * lam + (below + vert[z])
        return [(base + s[0], None if s[1] is None else s[1] + jnp.zeros_like(lam)) for s in shifts]

    below = vert[last]
    carry = []
    for k, d in enumerate(diagonal(0, below)):
        inv = inverse(d)
        g = (below + jnp.zeros_like(lam), None)
        if k:
            g = (g[0], jnp.zeros_like(lam))
        store(inv_ref, k, 0, inv)
        store(resp_ref, k, 0, g)
        carry.append((inv, times(inv, g)))

    def flat(items):
        return tuple(jax.tree.leaves(items))

    tree = jax.tree.structure(carry)

    def forward(z, leaves):
        items = jax.tree.unflatten(tree, leaves)
        below = vert[z - 1]
        fresh = []
        for k, d in enumerate(diagonal(z, below)):
            inv, resp = items[k]
            inv = inverse(plus(d, scaled(-(below * below), inv)))
            g = scaled(below, resp)
            store(inv_ref, k, z, inv)
            store(resp_ref, k, z, g)
            fresh.append((inv, times(inv, g)))
        return flat(fresh)

    lax.fori_loop(1, last, forward, flat(carry))
    ones = jnp.ones_like(lam)
    start = [(ones, None if k == 0 else jnp.zeros_like(lam)) for k in range(NODES)]
    tree_up = jax.tree.structure(start)

    def upward(step, leaves):
        items = jax.tree.unflatten(tree_up, leaves)
        z = last - 1 - step
        above = vert[z]
        fresh = []
        for k in range(NODES):
            g = plus(load(resp_ref, k, z), scaled(above, items[k]))
            value = times(load(inv_ref, k, z), g)
            store(resp_ref, k, z, value)
            fresh.append(value)
        return flat(fresh)

    lax.fori_loop(0, last, upward, flat(start))
    for k, d in enumerate(diagonal(last, vert[last - 1])):
        d = plus(d, scaled(-vert[last - 1], load(resp_ref, k, last - 1)))
        d = plus(d, scaled(-vert[last], load(resp_ref, k, 0)))
        store(resp_ref, k, last, inverse(d))


def solve(src, dst, scale, vert, inv_ref, resp_ref, half_ref):
    layers = resp_ref.shape[1]
    last = layers - 1
    nodes = talbot_nodes(NODES)
    weights = [(n[2] * scale, n[3] * scale) for n in nodes]
    zero = jnp.zeros(src.shape[1:], jnp.float32)
    start = [(zero, None if k == 0 else zero) for k in range(NODES)]
    tree = jax.tree.structure(start)

    def flat(items):
        return tuple(jax.tree.leaves(items))

    def gather(z, leaves):
        items = jax.tree.unflatten(tree, leaves)
        value = (src[z], None)
        return flat([plus(items[k], times(load(resp_ref, k, z), value)) for k in range(NODES)])

    sums = jax.tree.unflatten(tree, lax.fori_loop(0, last, gather, flat(start)))
    rhs = src[last]
    roots = [times(load(resp_ref, k, last), plus(sums[k], (rhs, None))) for k in range(NODES)]

    def real_total(items):
        total = weights[0][0] * items[0][0]
        for k in range(1, NODES):
            total = total + weights[k][0] * items[k][0] - weights[k][1] * items[k][1]
        return total

    dst[last] = real_total(roots)

    def forward(z, leaves):
        items = jax.tree.unflatten(tree, leaves)
        below = vert[lax.select(z == 0, last, z - 1)]
        value = (src[z], None)
        fresh = []
        for k in range(NODES):
            g = plus(scaled(below, items[k]), value)
            store(half_ref, k, z, g)
            fresh.append(times(load(inv_ref, k, z), g))
        return flat(fresh)

    lax.fori_loop(0, last, forward, flat(roots))

    def downward(step, leaves):
        items = jax.tree.unflatten(tree, leaves)
        z = last - 1 - step
        above = vert[z]
        fresh = []
        for k in range(NODES):
            g = plus(load(half_ref, k, z), scaled(above, items[k]))
            fresh.append(times(load(inv_ref, k, z), g))
        dst[z] = real_total(fresh)
        return flat(fresh)

    lax.fori_loop(0, last, downward, flat(roots))


def solve_kernel(scale, src, lam, lat, vert, dst, inv_ref, resp_ref, half_ref):
    factor(lam[...], lat, vert, inv_ref, resp_ref)
    solve(src, dst, scale, vert, inv_ref, resp_ref, half_ref)


def vertical_solves(source, lam, lateral, vertical, scale):
    layers, rows, width = source.shape
    plane = (PLANES, layers, rows, width)
    return pl.pallas_call(
        functools.partial(solve_kernel, scale),
        out_shape=jax.ShapeDtypeStruct(source.shape, jnp.float32),
        in_specs=[pl.BlockSpec(memory_space=pltpu.VMEM)] * 2
        + [pl.BlockSpec(memory_space=pltpu.SMEM)] * 2,
        out_specs=pl.BlockSpec(memory_space=pltpu.VMEM),
        scratch_shapes=[pltpu.VMEM(plane, jnp.float32)] * 3,
        compiler_params=pltpu.CompilerParams(vmem_limit_bytes=50 * 1024 * 1024),
    )(source, lam, lateral, vertical)


def plain_path(initial, lateral, vertical):
    z_cells, x_local, y_width = initial.shape
    tr_count, line_count = lax.axis_size("tr"), lax.axis_size("line")
    peers = tr_count * line_count
    x_width = x_local * tr_count
    layers = z_cells * line_count
    y_local = y_width // peers
    high = lax.Precision.HIGH
    along_y = jnp.asarray(hartley(y_width), jnp.float32)
    along_x = jnp.asarray(hartley(x_width), jnp.float32)
    me = lax.axis_index(AXES)
    modes = jnp.einsum("zxy,qy->zqx", initial, along_y, precision=high)
    modes = modes.reshape(z_cells, peers, y_local, x_local).transpose(1, 0, 2, 3)
    modes = lax.all_to_all(modes, AXES, split_axis=0, concat_axis=0, tiled=True)
    modes = modes.reshape(line_count, tr_count, z_cells, y_local, x_local)
    modes = modes.transpose(0, 2, 3, 1, 4).reshape(layers, y_local, x_width)
    modes = jnp.einsum("zqx,xp->zqp", modes, along_x, precision=high)
    lam_y = lax.dynamic_slice_in_dim(
        jnp.asarray(mode_values(y_width), jnp.float32), me * y_local, y_local
    )
    lam = lam_y[:, None] + jnp.asarray(mode_values(x_width), jnp.float32)[None, :]
    total = vertical_solves(modes, lam, lateral, vertical, 1.0 / (x_width * y_width))
    back = jnp.einsum("zqp,px->zqx", total, along_x, precision=high)
    back = back.reshape(line_count, z_cells, y_local, tr_count, x_local)
    back = back.transpose(0, 3, 1, 2, 4).reshape(peers, z_cells, y_local, x_local)
    back = lax.all_to_all(back, AXES, split_axis=0, concat_axis=0, tiled=True)
    back = back.transpose(1, 0, 2, 3).reshape(z_cells, y_width, x_local)
    return jnp.einsum("zqx,qy->zxy", back, along_y, precision=high)


def split(value):
    high = value.astype(jnp.bfloat16)
    return high, (value - high.astype(jnp.float32)).astype(jnp.bfloat16)


def three_pass(left, right, dims):
    def dot(a, b):
        return lax.dot_general(a, b, (dims, ((), ())), preferred_element_type=jnp.float32)

    return dot(left[0], right[0]) + (dot(left[1], right[0]) + dot(left[0], right[1]))


ROWS = 8


def fused_kernel(
    scale,
    sizes,
    init_hbm,
    y_hbm,
    x_hbm,
    lam_hbm,
    faces_hbm,
    out,
    init,
    y_pair,
    x_pair,
    lam,
    faces,
    sent,
    arrived,
    modes,
    solved,
    replies,
    back,
    inv_ref,
    resp_ref,
    half_ref,
    load_sem,
    send_sem,
    recv_sem,
):
    line_count, tr_count, chunks = sizes
    peers = line_count * tr_count
    z_cells, x_local, y_width = init.shape
    x_width = x_local * tr_count
    layers = z_cells * line_count
    band = peers * ROWS
    line, tr = lax.axis_index("line"), lax.axis_index("tr")
    me = line * tr_count + tr

    def loading(place, source, target):
        return pltpu.make_async_copy(source, target, load_sem.at[place])

    first_loads = [loading(0, init_hbm, init), loading(1, y_hbm, y_pair)]
    later_loads = [loading(2, faces_hbm, faces)]
    lat, vert = faces.at[0], faces.at[1]
    for h in range(chunks):
        own = pl.multiple_of(h * band + me * ROWS, ROWS)
        later_loads.append(loading(4 + h, lam_hbm.at[pl.ds(own, ROWS), :], lam.at[h]))
    if x_hbm is y_hbm:
        x_pair = y_pair
    else:
        later_loads.append(loading(4 + chunks, x_hbm, x_pair))
    for copy in first_loads + later_loads:
        copy.start()

    def place(index):
        return {"line": index // tr_count, "tr": lax.rem(index, tr_count)}

    def after(j):
        return lax.rem(me + j, peers)

    def before(j):
        return lax.rem(me + peers - j, peers)

    def block(ref, h, index):
        first = pl.multiple_of((index // tr_count) * z_cells, z_cells)
        column = pl.multiple_of(lax.rem(index, tr_count) * x_local, x_local)
        return ref.at[h, pl.ds(first, z_cells), :, pl.ds(column, x_local)]

    def rows(ref, h, index):
        return ref.at[h, :, pl.ds(pl.multiple_of(index * ROWS, ROWS), ROWS), :]

    def forth(h, src_index, dst_index, j):
        return pltpu.make_async_remote_copy(
            src_ref=rows(sent, h, dst_index),
            dst_ref=block(arrived, h, src_index),
            send_sem=send_sem.at[0, h, j],
            recv_sem=recv_sem.at[0, h, j],
            device_id=place(dst_index),
            device_id_type=pl.DeviceIdType.MESH,
        )

    def reply(h, src_index, dst_index, j):
        return pltpu.make_async_remote_copy(
            src_ref=block(replies, h, dst_index),
            dst_ref=rows(back, h, src_index),
            send_sem=send_sem.at[1, h, j],
            recv_sem=recv_sem.at[1, h, j],
            device_id=place(dst_index),
            device_id_type=pl.DeviceIdType.MESH,
        )

    def start_all(make, h):
        @pl.loop(1, peers)
        def _(j):
            make(h, me, after(j), j).start()

    def receive_all(make, h):
        @pl.loop(1, peers)
        def _(j):
            make(h, before(j), me, j).wait_recv()

    def sent_all(make, h):
        @pl.loop(1, peers)
        def _(j):
            make(h, me, after(j), j).wait_send()

    barrier = pltpu.get_barrier_semaphore()

    @pl.loop(1, peers)
    def _(j):
        pl.semaphore_signal(
            barrier, inc=1, device_id=place(after(j)), device_id_type=pl.DeviceIdType.MESH
        )

    for copy in first_loads:
        copy.wait()
    source = split(init[...].reshape(z_cells * x_local, y_width))
    for h in range(chunks):
        part = (y_pair[0, pl.ds(h * band, band), :], y_pair[1, pl.ds(h * band, band), :])
        spectrum = three_pass(part, source, ((1,), (1,)))
        for z in range(z_cells):
            sent[h, z] = spectrum[:, z * x_local : (z + 1) * x_local]
        if h == 0:
            pl.semaphore_wait(barrier, peers - 1)
        start_all(forth, h)
    for h in range(chunks):
        block(arrived, h, me)[...] = rows(sent, h, me)[...]
    for copy in later_loads:
        copy.wait()
    for h in range(chunks):
        factor(lam[h], lat, vert, inv_ref.at[h], resp_ref.at[h])
    x_pair = (x_pair[0], x_pair[1])
    for h in range(chunks):
        receive_all(forth, h)
        flat = split(arrived[h].reshape(layers * ROWS, x_width))
        modes[...] = three_pass(flat, x_pair, ((1,), (0,))).reshape(layers, ROWS, x_width)
        solve(modes, solved, scale, vert, inv_ref.at[h], resp_ref.at[h], half_ref)
        flat = split(solved[...].reshape(layers * ROWS, x_width))
        replies[h] = three_pass(flat, x_pair, ((1,), (0,))).reshape(layers, ROWS, x_width)
        start_all(reply, h)
        rows(back, h, me)[...] = block(replies, h, me)[...]
    for h in range(chunks):
        receive_all(reply, h)
        part = (y_pair[0, pl.ds(h * band, band), :], y_pair[1, pl.ds(h * band, band), :])
        wide = jnp.concatenate([back[h, z] for z in range(z_cells)], axis=1)
        field = three_pass(split(wide.T), part, ((1,), (0,)))
        field = field.reshape(z_cells, x_local, y_width)
        if h == 0:
            out[...] = field
        else:
            out[...] += field
    for h in range(chunks):
        sent_all(forth, h)
        sent_all(reply, h)


def halves(matrix):
    single = np.asarray(matrix, np.float32)
    high = single.astype(jnp.bfloat16)
    return high, (single - high.astype(np.float32)).astype(jnp.bfloat16)


def fused_path(initial, lateral, vertical):
    z_cells, x_local, y_width = initial.shape
    tr_count, line_count = lax.axis_size("tr"), lax.axis_size("line")
    peers = tr_count * line_count
    x_width = x_local * tr_count
    layers = z_cells * line_count
    chunks = y_width // (peers * ROWS)
    y_pair = np.stack(halves(hartley(y_width)))
    matrices = [jnp.asarray(y_pair)]
    if x_width != y_width:
        matrices.append(jnp.asarray(np.stack(halves(hartley(x_width)))))
    lam = mode_values(y_width)[:, None] + mode_values(x_width)[None, :]
    f32 = jnp.float32
    scratch_x = (2, x_width, x_width) if x_width != y_width else (2, 16, 128)
    narrow = pltpu.VMEM((chunks, z_cells, peers * ROWS, x_local), f32)
    whole = pltpu.VMEM((chunks, layers, ROWS, x_width), f32)
    one = pltpu.VMEM((layers, ROWS, x_width), f32)
    planes = pltpu.VMEM((chunks, PLANES, layers, ROWS, x_width), f32)
    body = functools.partial(
        fused_kernel, 1.0 / (x_width * y_width), (line_count, tr_count, chunks)
    )

    def kernel(init, y_ref, *rest):
        if len(matrices) == 1:
            rest = (y_ref,) + rest
        body(init, y_ref, *rest)

    return pl.pallas_call(
        kernel,
        out_shape=jax.ShapeDtypeStruct(initial.shape, f32),
        in_specs=[pl.BlockSpec(memory_space=pltpu.HBM)] * (3 + len(matrices)),
        out_specs=pl.BlockSpec(memory_space=pltpu.VMEM),
        scratch_shapes=[
            pltpu.VMEM(initial.shape, f32),
            pltpu.VMEM(y_pair.shape, jnp.bfloat16),
            pltpu.VMEM(scratch_x, jnp.bfloat16),
            pltpu.VMEM((chunks, ROWS, x_width), f32),
            pltpu.SMEM((2, layers), f32),
            narrow,
            whole,
            one,
            one,
            whole,
            narrow,
            planes,
            planes,
            pltpu.VMEM((PLANES, layers, ROWS, x_width), f32),
            pltpu.SemaphoreType.DMA((5 + chunks,)),
            pltpu.SemaphoreType.DMA((2, chunks, peers)),
            pltpu.SemaphoreType.DMA((2, chunks, peers)),
        ],
        compiler_params=pltpu.CompilerParams(
            collective_id=0, has_side_effects=True, vmem_limit_bytes=52 * 1024 * 1024
        ),
        cost_estimate=pl.CostEstimate(
            flops=24 * z_cells * x_local * y_width * y_width,
            bytes_accessed=12 * z_cells * x_local * y_width,
            transcendentals=0,
        ),
    )(
        initial,
        *matrices,
        jnp.asarray(lam, f32),
        jnp.stack([lateral, vertical]),
    )


def local(initial, lateral, vertical):
    z_cells, x_local, y_width = initial.shape
    peers = lax.axis_size("tr") * lax.axis_size("line")
    if x_local % 128 == 0 and y_width % (peers * ROWS) == 0:
        return fused_path(initial, lateral, vertical)
    return plain_path(initial, lateral, vertical)


def solution(mesh):
    in_specs = (P("line", "tr", None), P(), P())
    out_specs = P("line", "tr", None)
    return jax.shard_map(
        local, mesh=mesh, in_specs=in_specs, out_specs=out_specs, check_vma=False
    )
```
